32 devices in a mesh: dp: 4 (over y, x), seq: 4 (over z), expert: 2 (over core).
Axes of the slice: x: 2, y: 2, z: 4, core: 2. Of those that a mesh axis runs over, the one named last changes fastest.
Arguments:
- frames: bfloat16 [8, 512, 1024], P(('dp', 'expert'), 'seq'), may hold values from -6 to 6
- lengths: int32 [8], P(('dp', 'expert')), may hold values from 128 to 512, as said below
- routes: int32 [8, 512, 2], P(('dp', 'expert'), 'seq'), may hold values from 0 to 7, all different within a row; in each aligned block of 128 rows (0 to 127, 128 to 255, ..., all dimensions but the last counted through in order) at most 48 rows name the same one
- norm_conv: float32 [1024], replicated, may hold values from 0.1 to 1.9
- point_in: bfloat16 [1024, 2048], replicated, may hold values from -0.1875 to 0.1875
- depth_kernel: float32 [31, 1024], replicated, may hold values from -1 to 1
- bn_scale: float32 [1024], replicated, may hold values from 0.1 to 1.9
- bn_shift: float32 [1024], replicated, may hold values from -3 to 3
- point_out: bfloat16 [1024, 1024], replicated, may hold values from -0.1875 to 0.1875
- norm_moe: float32 [1024], replicated, may hold values from 0.1 to 1.9
- router: bfloat16 [1024, 8], replicated, may hold values from -0.1875 to 0.1875
- gate_weight: bfloat16 [8, 1024, 4096], P(('seq', 'expert'), None, 'dp'), may hold values from -0.1875 to 0.1875
- up_weight: bfloat16 [8, 1024, 4096], P(('seq', 'expert'), None, 'dp'), may hold values from -0.1875 to 0.1875
- down_weight: bfloat16 [8, 1024, 4096], P(('seq', 'expert'), None, 'dp'), may hold values from -0.09375 to 0.09375
Outputs:
- layer_out: bfloat16 [8, 512, 1024], P(('dp', 'expert'), 'seq')
The draws below stay inside these ranges and needn't reach their ends.
Inputs may be any that keep to these rules, and one draw needn't show every extreme that they name: `lengths`: each utterance has between 128 and 512 valid frames; some utterance has all 512, some only 128. `routes`: the two experts of a frame differ. Among the 128 frames of one device (aligned blocks of frames of one utterance), no expert is named more than 48 times, and in some blocks one expert is named exactly 48 times. Padded frames are routed too.
All inputs are finite; a program needn't handle non-finite values.
Results may differ from the reference program's by a relative error of at most 0.0085.
Values may be sent and summed in bfloat16 or wider, within the bound.
A program may use at most 128 MiB of HBM per device.

```python
import math
import jax
import jax.numpy as jnp
import numpy as np
from jax import lax

D = 1024
FF = 4096
KERNEL = 31
TOK_DEV = 128
EXPERTS = 8
CAP = 48
FRAMES = 512
UTTS = 8


def draw_lengths(key, part):
    shorter = FRAMES // 4
    values = jax.random.randint(jax.random.fold_in(key, 11), (UTTS,), shorter, FRAMES + 1, dtype=jnp.int32)
    order = jax.random.permutation(jax.random.fold_in(key, 12), UTTS)
    values = values.at[order[0]].set(FRAMES)
    values = values.at[order[1]].set(shorter)
    return values


def steps_of(stream_key, shape, split, smallest, largest):
    level, own = 1.0, jax.random.fold_in(stream_key, 6)
    for dim, parts in split:
        heights = jnp.exp(jax.random.uniform(jax.random.fold_in(own, dim), (parts,), jnp.float32, smallest / len(split), largest / len(split)))
        level = level * jnp.repeat(heights, shape[dim] // parts).reshape([-1 if axis == dim else 1 for axis in range(len(shape))])
    return level


def routed_block(rng, own, number, rows, number_of, top, bound, slope):
    order = jax.random.permutation(rng, number_of)
    crowded, common = portions_of(number_of, rows * top, bound, slope, True), portions_of(number_of, rows * top, bound, slope, False)
    places = jnp.arange(number_of)

    def named(sizes, turn):
        used = int((sizes > 0).sum())
        fixed = max(1, used // 4)
        shifted = fixed + (places - fixed + turn * (used - fixed)) % max(1, number_of - fixed)
        return jnp.zeros((number_of,), jnp.int32).at[order[jnp.where(places < fixed, places, shifted)]].set(jnp.asarray(sizes, jnp.int32))

    sizes = jnp.where(number % 4 == 0, named(crowded, number // 4), named(common, number - number // 4 - 1))
    mixed = jax.random.permutation(jax.random.fold_in(own, 3), number_of)
    source_of, sink = mixed[0:number_of // 2 * 2:2], mixed[1:number_of // 2 * 2:2]
    margin = jnp.minimum(sizes[source_of] - 1, bound - sizes[sink]) // 2
    margin = jnp.where((source_of == order[0]) | (sink == order[0]) | (sizes[sink] == 0), 0, jnp.maximum(margin, 0))
    shifted = jax.random.randint(jax.random.fold_in(own, 4), (number_of // 2,), 0, 1 << 20) % (margin + 1)
    sizes = sizes.at[source_of].add(-shifted).at[sink].add(shifted)
    members = jnp.searchsorted(jnp.cumsum(sizes), jnp.arange(rows * top), side="right").astype(jnp.int32)
    listing = members.reshape(top, rows).T
    listing = listing[jax.random.permutation(jax.random.fold_in(own, 1), rows)]
    turn = jax.random.randint(jax.random.fold_in(own, 2), (rows, 1), 0, top)
    return jnp.take_along_axis(listing, (jnp.arange(top)[None, :] + turn) % top, axis=1)


def portions_of(count, total, bound, slope, full):
    loads = [(1 << 20) // math.isqrt(rank ** slope) + 1 for rank in range(1, count + 1)]
    largest = bound if full else min(bound, max(-(-total // count), total * loads[0] // sum(loads)))
    least = 1 if total - largest >= count - 1 else 0
    counts, surplus = [largest] + [least] * (count - 1), total - largest - least * (count - 1)
    while surplus > 0:
        free = [i for i in range(1, count) if counts[i] < largest] or [i for i in range(1, count) if counts[i] < bound]
        whole, budget = sum([loads[i] for i in free]), surplus
        for i in free:
            addition = min(bound - counts[i], max(1, budget * loads[i] // whole), surplus)
            counts[i] = counts[i] + addition
            surplus = surplus - addition
    return np.array(counts)


def gaussian(key, extent, scale, limit, split=(), kind=jnp.bfloat16):
    loudness = steps_of(key, extent, split, -0.22, 0.18) if split else 1.0
    values = jax.random.normal(key, extent, jnp.float32) * scale * loudness
    return jnp.minimum(jnp.maximum(values, -limit), limit).astype(kind)


def setup_inputs(seed: int = 0) -> dict:
    seeds = jax.random.split(jax.random.key(seed), 15)
    frames = gaussian(seeds[0], (UTTS, FRAMES, D), 1.0, 6.0, ((0, 8), (1, 4)))
    lengths = draw_lengths(jax.random.fold_in(seeds[14], 71), 0)
    routes_keys = jax.random.split(jax.random.fold_in(seeds[2], 1), UTTS * FRAMES // TOK_DEV)
    routes_turns = jax.random.permutation(jax.random.fold_in(seeds[2], 3), UTTS * FRAMES // TOK_DEV)
    routes = jax.vmap(lambda own, number: routed_block(jax.random.fold_in(seeds[2], 2), own, number, TOK_DEV, EXPERTS, 2, CAP, 2))(routes_keys, routes_turns).reshape((UTTS, FRAMES, 2))
    norm_conv = jnp.clip(1.0 + 0.18 * jax.random.normal(seeds[3], (D,), jnp.float32), 0.1, 1.9)
    point_in = gaussian(seeds[4], (D, 2 * D), D ** -0.5, 0.1875)
    depth_kernel = gaussian(seeds[5], (KERNEL, D), KERNEL ** -0.5, 1.0, (), jnp.float32)
    bn_scale = jnp.clip(1.0 + 0.18 * jax.random.normal(seeds[6], (D,), jnp.float32), 0.1, 1.9)
    bn_shift = gaussian(seeds[7], (D,), 0.5, 3.0, (), jnp.float32)
    point_out = gaussian(seeds[8], (D, D), D ** -0.5, 0.1875)
    norm_moe = jnp.clip(1.0 + 0.18 * jax.random.normal(seeds[9], (D,), jnp.float32), 0.1, 1.9)
    router = gaussian(seeds[10], (D, EXPERTS), D ** -0.5, 0.1875)
    gate_weight = gaussian(seeds[11], (EXPERTS, D, FF), D ** -0.5, 0.1875, ((0, 8), (2, 4)))
    up_weight = gaussian(seeds[12], (EXPERTS, D, FF), D ** -0.5, 0.1875, ((0, 8), (2, 4)))
    down_weight = gaussian(seeds[13], (EXPERTS, D, FF), FF ** -0.5, 0.09375, ((0, 8), (2, 4)))
    return {"frames": frames, "lengths": lengths, "routes": routes, "norm_conv": norm_conv, "point_in": point_in, "depth_kernel": depth_kernel, "bn_scale": bn_scale, "bn_shift": bn_shift, "point_out": point_out, "norm_moe": norm_moe, "router": router, "gate_weight": gate_weight, "up_weight": up_weight, "down_weight": down_weight}


def layer_norm(values, gain):
    values = values.astype(jnp.float32)
    center = values - lax.optimization_barrier(jnp.mean(values, axis=-1, keepdims=True))
    spread = lax.optimization_barrier(jnp.mean(center * center, axis=-1, keepdims=True))
    return center * lax.rsqrt(spread + 1e-05) * gain

def reference(frames, lengths, routes, norm_conv, point_in, depth_kernel, bn_scale, bn_shift, point_out, norm_moe, router, gate_weight, up_weight, down_weight):
    utt_count, frame_count, model_width = frames.shape
    total_rows = utt_count * frame_count
    position = jnp.arange(frame_count, dtype=jnp.int32)
    frame_mask = (position[None, :] < lengths[:, None]).astype(jnp.float32).reshape(total_rows, 1)
    flat_in = frames.reshape(total_rows, model_width)
    conv_in = layer_norm(flat_in, norm_conv).astype(jnp.bfloat16)
    lifted = jnp.dot(conv_in.astype(jnp.float32), point_in.astype(jnp.float32), preferred_element_type=jnp.float32)
    gated = (lifted[:, :model_width] * jax.nn.sigmoid(lifted[:, model_width:]) * frame_mask).astype(jnp.bfloat16)
    gated = gated.reshape(utt_count, frame_count, model_width)
    reach = depth_kernel.shape[0] // 2
    padded = jnp.pad(gated, ((0, 0), (reach, reach), (0, 0)))
    depth = jnp.zeros((utt_count, frame_count, model_width), jnp.float32)
    for offset in range(depth_kernel.shape[0]):
        depth = depth + padded[:, offset:offset + frame_count].astype(jnp.float32) * depth_kernel[offset]
    swished = jax.nn.silu(depth * bn_scale + bn_shift).astype(jnp.bfloat16).reshape(total_rows, model_width)
    residual = flat_in.astype(jnp.float32) + jnp.dot(swished.astype(jnp.float32), point_out.astype(jnp.float32), preferred_element_type=jnp.float32)
    moe_in = layer_norm(residual, norm_moe).astype(jnp.bfloat16)
    logits = jnp.dot(moe_in.astype(jnp.float32), router.astype(jnp.float32), preferred_element_type=jnp.float32)
    choice_ids = routes.reshape(total_rows, 2).astype(jnp.int32)
    picked = jnp.take_along_axis(logits, choice_ids, axis=1)
    weight_one = jax.nn.sigmoid(picked[:, 0] - picked[:, 1])
    weight_two = jax.nn.sigmoid(picked[:, 1] - picked[:, 0])
    expert_ids = jnp.arange(EXPERTS, dtype=jnp.int32)
    pick_one = (choice_ids[:, 0:1] == expert_ids[None, :]).astype(jnp.int32)
    pick_two = (choice_ids[:, 1:2] == expert_ids[None, :]).astype(jnp.int32)
    both = (pick_one + pick_two).reshape(total_rows // TOK_DEV, TOK_DEV, EXPERTS)
    earlier = (jnp.cumsum(both, axis=1) - both).reshape(total_rows, EXPERTS)
    slot_one = lax.optimization_barrier(jnp.sum(earlier * pick_one, axis=1))
    slot_two = lax.optimization_barrier(jnp.sum(earlier * pick_two, axis=1))
    row_ids = jnp.arange(total_rows, dtype=jnp.int32)
    block_base = row_ids // TOK_DEV * CAP
    slot_count = total_rows // TOK_DEV * CAP
    table = jnp.full((EXPERTS, slot_count), total_rows, jnp.int32)
    table = table.at[choice_ids[:, 0], block_base + slot_one].set(row_ids)
    table = table.at[choice_ids[:, 1], block_base + slot_two].set(row_ids)
    weights_table = jnp.zeros((EXPERTS, slot_count), jnp.float32)
    weights_table = weights_table.at[choice_ids[:, 0], block_base + slot_one].set(weight_one)
    weights_table = weights_table.at[choice_ids[:, 1], block_base + slot_two].set(weight_two)
    padded_in = jnp.concatenate([moe_in, jnp.zeros((1, model_width), jnp.bfloat16)], axis=0)

    def one_expert(accum, inputs):
        indices, slot_weights, gate_one, up_one, down_one = inputs
        chosen = padded_in[indices].astype(jnp.float32)
        gate_part = jnp.dot(chosen, gate_one.astype(jnp.float32), preferred_element_type=jnp.float32)
        up_part = jnp.dot(chosen, up_one.astype(jnp.float32), preferred_element_type=jnp.float32)
        hidden = (jax.nn.silu(gate_part) * up_part).astype(jnp.bfloat16)
        expert_out = jnp.dot(hidden.astype(jnp.float32), down_one.astype(jnp.float32).T, preferred_element_type=jnp.float32).astype(jnp.bfloat16)
        accum = accum.at[indices].add(slot_weights[:, None] * expert_out.astype(jnp.float32))
        return (accum, None)
    accum, unused = lax.scan(one_expert, jnp.zeros((total_rows + 1, model_width), jnp.float32), (table, weights_table, gate_weight, up_weight, down_weight))
    layer_out = ((residual + accum[:total_rows]) * frame_mask).astype(jnp.bfloat16)
    return layer_out.reshape(utt_count, frame_count, model_width)
```

```python
import functools
import jax
import jax.numpy as jnp
from jax import lax
from jax.experimental import pallas as pl
from jax.experimental.pallas import tpu as pltpu
from jax.sharding import PartitionSpec as P


def padded_2(x, sides, width):
    for axis, dim in sides:
        size, length = (lax.axis_size(axis), x.shape[dim])
        up = [(i, (i + 1) % size) for i in range(size - 1)]
        down = [(j, i) for i, j in up]
        last = lax.slice_in_dim(x, length - width, length, axis=dim)
        initial = lax.slice_in_dim(x, 0, width, axis=dim)
        before = lax.ppermute(last, axis, up)
        after = lax.ppermute(initial, axis, down)
        x = jnp.concatenate([before, x, after], axis=dim)
    return x


def layer_norm(values, gain):
    values = values.astype(jnp.float32)
    center = values - jnp.mean(values, axis=-1, keepdims=True)
    spread = jnp.mean(center * center, axis=-1, keepdims=True)
    return center * lax.rsqrt(spread + 1e-05) * gain


MESH = pl.DeviceIdType.MESH


def kernel_fits(token_count, model_width, capacity, hidden):
    sizes = (lax.axis_size("dp"), lax.axis_size("expert"))
    return sizes == (4, 2) and capacity % 16 == 0 and model_width % 256 == 0 and hidden % 256 == 0


def exchange_kernel(
    seq,
    out_hbm,
    gate_hbm,
    up_hbm,
    down_hbm,
    back,
    sent,
    gate,
    up,
    down,
    rows,
    part,
    half,
    joined,
    sums,
    total,
    hidden,
    load_sem,
    own_sem,
    z_send,
    z_recv,
    g_send,
    g_recv,
    r_send,
    r_recv,
    b_send,
    b_recv,
):
    d, s, c = lax.axis_index("dp"), lax.axis_index("seq"), lax.axis_index("expert")
    other = 1 - c
    cap, width = rows.shape[3], rows.shape[4]
    along_x = (d // 2 * 2 + (1 - d % 2), s, c)
    along_y = ((d + 2) % 4, s, c)
    loads = [
        pltpu.make_async_copy(out_hbm, sent, load_sem.at[0]),
        pltpu.make_async_copy(gate_hbm, gate, load_sem.at[1]),
        pltpu.make_async_copy(up_hbm, up, load_sem.at[2]),
        pltpu.make_async_copy(down_hbm, down, load_sem.at[3]),
    ]
    for load in loads:
        load.start()

    barrier = pltpu.get_barrier_semaphore()
    peers = [along_x, along_y, (d, s, other)]
    for k in range(1, seq):
        peers += [(d, (s + k) % seq, 0), (d, (s + k) % seq, 1)]
    for peer in peers:
        pl.semaphore_signal(barrier, inc=1, device_id=peer, device_id_type=MESH)
    pl.semaphore_wait(barrier, len(peers))
    loads[0].wait()

    def remote(src, dst, send, recv, to):
        return pltpu.make_async_remote_copy(
            src_ref=src, dst_ref=dst, send_sem=send, recv_sem=recv, device_id=to, device_id_type=MESH
        )

    def z_copy(k, q):
        to = (s + seq - k) % seq
        return remote(
            sent.at[2 * to + q], rows.at[k, 0, c], z_send.at[k, q], z_recv.at[k, c], (d, to, q)
        )

    def z_arrival(k, q):
        return remote(sent.at[0], rows.at[k, 0, q], z_send.at[k, q], z_recv.at[k, q], (d, s, other))

    own = pltpu.make_async_copy(sent.at[2 * s + c], rows.at[0, 0, c], own_sem.at[0])
    own.start()
    z_copy(0, other).start()
    for k in range(1, seq):
        z_copy(k, 0).start()
        z_copy(k, 1).start()

    def g_x(k):
        return remote(rows.at[k, 0], rows.at[k, 1], g_send.at[k, 0], g_recv.at[k, 0], along_x)

    def g_y(k):
        return remote(rows.at[k, 0], rows.at[k, 2], g_send.at[k, 1], g_recv.at[k, 1], along_y)

    def g_xy(k):
        return remote(rows.at[k, 1, 0], rows.at[k, 3, 0], g_send.at[k, 2], g_recv.at[k, 2], along_y)

    def g_yx(k):
        return remote(rows.at[k, 2, 1], rows.at[k, 3, 1], g_send.at[k, 3], g_recv.at[k, 3], along_x)

    def r_xy(k):
        return remote(part.at[k, 3, 0], half.at[k, 0], r_send.at[k, 0], r_recv.at[k, 0], along_x)

    def r_yx(k):
        return remote(part.at[k, 3, 1], half.at[k, 1], r_send.at[k, 1], r_recv.at[k, 1], along_y)

    def r_x(k):
        return remote(part.at[k, 1, 0], sums.at[k, 0, 0], r_send.at[k, 2], r_recv.at[k, 2], along_x)

    def r_y(k):
        return remote(part.at[k, 2, 1], sums.at[k, 1, 1], r_send.at[k, 3], r_recv.at[k, 3], along_y)

    def r_x_joined(k):
        return remote(joined.at[k, 0], sums.at[k, 0, 1], r_send.at[k, 4], r_recv.at[k, 4], along_x)

    def r_y_joined(k):
        return remote(joined.at[k, 1], sums.at[k, 1, 0], r_send.at[k, 5], r_recv.at[k, 5], along_y)

    def b_copy(k, q):
        return remote(
            total.at[k, q], back.at[2 * s + c], b_send.at[k, q], b_recv.at[k, c], (d, (s + k) % seq, q)
        )

    def b_arrival(k, q):
        e = 2 * ((s + seq - k) % seq) + q
        return remote(total.at[k, q], back.at[e], b_send.at[k, q], b_recv.at[k, q], (d, s, other))

    own_back = pltpu.make_async_copy(total.at[0, c], back.at[2 * s + c], own_sem.at[1])

    def spread(k):
        @pl.when(k == 0)
        def _():
            own.wait()
            z_arrival(0, other).wait_recv()

        @pl.when(k > 0)
        def _():
            z_arrival(k, 0).wait_recv()
            z_arrival(k, 1).wait_recv()

        g_x(k).start()
        g_y(k).start()

    def pass_on(k):
        g_x(k).wait_recv()
        g_xy(k).start()
        g_y(k).wait_recv()
        g_yx(k).start()

    def experts(k):
        g_xy(k).wait_recv()
        g_yx(k).wait_recv()

        @pl.when(k == 0)
        def _():
            for load in loads[1:]:
                load.wait()

        @pl.loop(0, hidden.shape[1] // 256)
        def _(n):
            columns = pl.ds(pl.multiple_of(n * 256, 256), 256)
            x = rows[k].reshape(8 * cap, width)
            g = jnp.dot(x, gate[:, columns], preferred_element_type=jnp.float32)
            u = jnp.dot(x, up[:, columns], preferred_element_type=jnp.float32)
            hidden[:, columns] = (g / (1.0 + jnp.exp(-g)) * u).astype(jnp.bfloat16)

        @pl.loop(0, width // 256)
        def _(n):
            columns = pl.ds(pl.multiple_of(n * 256, 256), 256)
            y = lax.dot_general(
                hidden[...],
                down[columns, :],
                (((1,), (1,)), ((), ())),
                preferred_element_type=jnp.float32,
            )
            part[k, :, :, :, columns] = y.astype(jnp.bfloat16).reshape(4, 2, cap, 256)

        r_xy(k).start()
        r_yx(k).start()
        r_x(k).start()
        r_y(k).start()

    def join(k):
        r_yx(k).wait_recv()
        joined[k, 0] = (
            part[k, 1, 1].astype(jnp.float32) + half[k, 1].astype(jnp.float32)
        ).astype(jnp.bfloat16)
        r_x_joined(k).start()
        r_xy(k).wait_recv()
        joined[k, 1] = (
            part[k, 2, 0].astype(jnp.float32) + half[k, 0].astype(jnp.float32)
        ).astype(jnp.bfloat16)
        r_y_joined(k).start()

    def give_back(k):
        r_x(k).wait_recv()
        r_y(k).wait_recv()
        r_x_joined(k).wait_recv()
        r_y_joined(k).wait_recv()
        total[k] = (
            part[k, 0].astype(jnp.float32)
            + sums[k, 0].astype(jnp.float32)
            + sums[k, 1].astype(jnp.float32)
        ).astype(jnp.bfloat16)

        @pl.when(k == 0)
        def _():
            own_back.start()
            b_copy(0, other).start()

        @pl.when(k > 0)
        def _():
            b_copy(k, 0).start()
            b_copy(k, 1).start()

    def at(k, step):
        pl.when(jnp.logical_and(k >= 0, k < seq))(lambda: step(k))

    @pl.loop(0, seq + 4)
    def _(t):
        at(t, spread)
        at(t - 1, pass_on)
        at(t - 2, experts)
        at(t - 3, join)
        at(t - 4, give_back)

    own_back.wait()
    b_arrival(0, other).wait_recv()
    z_copy(0, other).wait_send()
    b_copy(0, other).wait_send()
    for k in range(1, seq):
        for q in range(2):
            b_arrival(k, q).wait_recv()
            z_copy(k, q).wait_send()
            b_copy(k, q).wait_send()

    @pl.loop(0, seq)
    def _(k):
        for copy in (g_x, g_y, g_xy, g_yx, r_xy, r_yx, r_x, r_y, r_x_joined, r_y_joined):
            copy(k).wait_send()


def exchange(outgoing, gate_local, up_local, down_local):
    experts, cap, width = outgoing.shape
    seq, ff = lax.axis_size("seq"), gate_local.shape[1]
    bf16, dma = jnp.bfloat16, pltpu.SemaphoreType.DMA
    flops = 6 * 4 * experts * cap * width * ff
    return pl.pallas_call(
        functools.partial(exchange_kernel, seq),
        out_shape=jax.ShapeDtypeStruct(outgoing.shape, bf16),
        in_specs=[pl.BlockSpec(memory_space=pl.ANY)] * 4,
        out_specs=pl.BlockSpec(memory_space=pltpu.VMEM),
        scratch_shapes=[
            pltpu.VMEM(outgoing.shape, bf16),
            pltpu.VMEM(gate_local.shape, bf16),
            pltpu.VMEM(up_local.shape, bf16),
            pltpu.VMEM(down_local.shape, bf16),
            pltpu.VMEM((seq, 4, 2, cap, width), bf16),
            pltpu.VMEM((seq, 4, 2, cap, width), bf16),
            pltpu.VMEM((seq, 2, cap, width), bf16),
            pltpu.VMEM((seq, 2, cap, width), bf16),
            pltpu.VMEM((seq, 2, 2, cap, width), bf16),
            pltpu.VMEM((seq, 2, cap, width), bf16),
            pltpu.VMEM((8 * cap, ff), bf16),
            dma((4,)),
            dma((2,)),
            dma((seq, 2)),
            dma((seq, 2)),
            dma((seq, 4)),
            dma((seq, 4)),
            dma((seq, 6)),
            dma((seq, 6)),
            dma((seq, 2)),
            dma((seq, 2)),
        ],
        compiler_params=pltpu.CompilerParams(
            collective_id=0, has_side_effects=True, vmem_limit_bytes=40 << 20
        ),
        cost_estimate=pl.CostEstimate(
            flops=flops, bytes_accessed=6 * width * ff, transcendentals=4 * experts * cap * ff
        ),
    )(outgoing, gate_local, up_local, down_local)


def exchange_plain(outgoing, gate_local, up_local, down_local):
    arrived = lax.all_to_all(outgoing, ("seq", "expert"), split_axis=0, concat_axis=0, tiled=True)
    arrived_shape = arrived.shape
    shard_rows = lax.all_gather(arrived.reshape(-1, arrived_shape[2]), "dp", axis=0, tiled=True)
    gate_part = jnp.dot(shard_rows, gate_local, preferred_element_type=jnp.float32)
    up_part = jnp.dot(shard_rows, up_local, preferred_element_type=jnp.float32)
    hidden = (jax.nn.silu(gate_part) * up_part).astype(jnp.bfloat16)
    summed = lax.psum_scatter(
        lax.dot_general(
            hidden, down_local, (((1,), (1,)), ((), ())), preferred_element_type=jnp.float32
        ).astype(jnp.bfloat16),
        "dp",
        scatter_dimension=0,
        tiled=True,
    )
    served = summed.reshape(arrived_shape)
    returned_rows = lax.all_to_all(
        served, ("seq", "expert"), split_axis=0, concat_axis=0, tiled=True
    )
    return returned_rows


def local(
    frames,
    lengths,
    routes,
    norm_conv,
    point_in,
    depth_kernel,
    bn_scale,
    bn_shift,
    point_out,
    norm_moe,
    router,
    gate_weight,
    up_weight,
    down_weight,
):
    frame_rows = frames[0]
    token_count = frame_rows.shape[0]
    model_width = frame_rows.shape[1]
    position = lax.axis_index("seq") * token_count + jnp.arange(token_count, dtype=jnp.int32)
    frame_mask = (position < lengths[0]).astype(jnp.float32)[:, None]
    conv_in = layer_norm(frame_rows, norm_conv).astype(jnp.bfloat16)
    lifted = jnp.dot(conv_in, point_in, preferred_element_type=jnp.float32)
    gated = (lifted[:, :model_width] * jax.nn.sigmoid(lifted[:, model_width:]) * frame_mask).astype(
        jnp.bfloat16
    )
    reach = depth_kernel.shape[0] // 2
    padded = padded_2(gated, (("seq", 0),), reach)
    depth = jnp.zeros((token_count, model_width), jnp.float32)
    for offset in range(depth_kernel.shape[0]):
        depth = (
            depth + padded[offset : offset + token_count].astype(jnp.float32) * depth_kernel[offset]
        )
    swished = jax.nn.silu(depth * bn_scale + bn_shift).astype(jnp.bfloat16)
    residual = frame_rows.astype(jnp.float32) + jnp.dot(
        swished, point_out, preferred_element_type=jnp.float32
    )
    moe_in = layer_norm(residual, norm_moe).astype(jnp.bfloat16)
    logits = jnp.dot(moe_in, router, preferred_element_type=jnp.float32)
    seq_count = lax.axis_size("seq")
    expert_count = seq_count * lax.axis_size("expert")
    capacity = 3 * token_count // expert_count
    choice_ids = routes[0]
    expert_ids = jnp.arange(expert_count, dtype=jnp.int32)
    pick_one = (choice_ids[:, 0:1] == expert_ids[None, :]).astype(jnp.int32)
    pick_two = (choice_ids[:, 1:2] == expert_ids[None, :]).astype(jnp.int32)
    logit_one = jnp.sum(logits * pick_one.astype(jnp.float32), axis=1)
    logit_two = jnp.sum(logits * pick_two.astype(jnp.float32), axis=1)
    weight_one = jax.nn.sigmoid(logit_one - logit_two)
    weight_two = jax.nn.sigmoid(logit_two - logit_one)
    both = pick_one + pick_two
    rank = jnp.arange(token_count, dtype=jnp.int32)
    lower = (rank[:, None] > rank[None, :]).astype(jnp.bfloat16)
    earlier = jnp.dot(
        lower, both.astype(jnp.bfloat16), preferred_element_type=jnp.float32
    ).astype(jnp.int32)
    place_one = choice_ids[:, 0] * capacity + jnp.sum(earlier * pick_one, axis=1)
    place_two = choice_ids[:, 1] * capacity + jnp.sum(earlier * pick_two, axis=1)
    slot_ids = jnp.arange(expert_count * capacity, dtype=jnp.int32)
    slot_one = (place_one[:, None] == slot_ids[None, :]).astype(jnp.bfloat16)
    slot_two = (place_two[:, None] == slot_ids[None, :]).astype(jnp.bfloat16)
    outgoing = lax.dot_general(
        slot_one + slot_two, moe_in, (((0,), (0,)), ((), ())), preferred_element_type=jnp.float32
    ).astype(jnp.bfloat16)
    outgoing = outgoing.reshape(expert_count, capacity, model_width)
    gate_local = gate_weight[0]
    up_local = up_weight[0]
    down_local = down_weight[0]
    if kernel_fits(token_count, model_width, capacity, gate_local.shape[1]):
        returned_rows = exchange(outgoing, gate_local, up_local, down_local)
    else:
        returned_rows = exchange_plain(outgoing, gate_local, up_local, down_local)
    returned_rows = returned_rows.reshape(expert_count * capacity, model_width)
    from_one = jnp.dot(slot_one, returned_rows, preferred_element_type=jnp.float32)
    from_two = jnp.dot(slot_two, returned_rows, preferred_element_type=jnp.float32)
    layer_out = (
        residual + weight_one[:, None] * from_one + weight_two[:, None] * from_two
    ) * frame_mask
    return layer_out.astype(jnp.bfloat16)[None]


def solution(mesh):
    return jax.shard_map(
        local,
        mesh=mesh,
        in_specs=(
            P(("dp", "expert"), "seq", None),
            P(("dp", "expert")),
            P(("dp", "expert"), "seq", None),
            P(),
            P(),
            P(),
            P(),
            P(),
            P(),
            P(),
            P(),
            P(("seq", "expert"), None, "dp"),
            P(("seq", "expert"), None, "dp"),
            P(("seq", "expert"), None, "dp"),
        ),
        out_specs=P(("dp", "expert"), "seq", None),
        check_vma=False,
    )
```

```python
import functools
import jax
import jax.numpy as jnp
from jax import lax
from jax.experimental import pallas as pl
from jax.experimental.pallas import tpu as pltpu
from jax.sharding import PartitionSpec as P


def padded_2(x, sides, width):
    for axis, dim in sides:
        size, length = (lax.axis_size(axis), x.shape[dim])
        up = [(i, (i + 1) % size) for i in range(size - 1)]
        down = [(j, i) for i, j in up]
        last = lax.slice_in_dim(x, length - width, length, axis=dim)
        initial = lax.slice_in_dim(x, 0, width, axis=dim)
        before = lax.ppermute(last, axis, up)
        after = lax.ppermute(initial, axis, down)
        x = jnp.concatenate([before, x, after], axis=dim)
    return x


def layer_norm(values, gain):
    values = values.astype(jnp.float32)
    center = values - jnp.mean(values, axis=-1, keepdims=True)
    spread = jnp.mean(center * center, axis=-1, keepdims=True)
    return center * lax.rsqrt(spread + 1e-05) * gain


MESH = pl.DeviceIdType.MESH


def kernel_fits(token_count, model_width, capacity, hidden):
    sizes = (lax.axis_size("dp"), lax.axis_size("expert"))
    return sizes == (4, 2) and capacity % 16 == 0 and model_width % 256 == 0 and hidden % 256 == 0


def exchange_kernel(
    seq,
    out_hbm,
    gate_hbm,
    up_hbm,
    down_hbm,
    back,
    sent,
    gate,
    up,
    down,
    rows,
    part,
    half,
    joined,
    sums,
    total,
    hidden,
    load_sem,
    own_sem,
    z_send,
    z_recv,
    g_send,
    g_recv,
    r_send,
    r_recv,
    b_send,
    b_recv,
):
    d, s, c = lax.axis_index("dp"), lax.axis_index("seq"), lax.axis_index("expert")
    other = 1 - c
    cap, width = rows.shape[3], rows.shape[4]
    along_x = (d // 2 * 2 + (1 - d % 2), s, c)
    along_y = ((d + 2) % 4, s, c)
    loads = [
        pltpu.make_async_copy(out_hbm, sent, load_sem.at[0]),
        pltpu.make_async_copy(gate_hbm, gate, load_sem.at[1]),
        pltpu.make_async_copy(up_hbm, up, load_sem.at[2]),
        pltpu.make_async_copy(down_hbm, down, load_sem.at[3]),
    ]
    for load in loads:
        load.start()

    barrier = pltpu.get_barrier_semaphore()
    peers = [along_x, along_y, (d, s, other)]
    for k in range(1, seq):
        peers += [(d, (s + k) % seq, 0), (d, (s + k) % seq, 1)]
    for peer in peers:
        pl.semaphore_signal(barrier, inc=1, device_id=peer, device_id_type=MESH)
    pl.semaphore_wait(barrier, len(peers))
    loads[0].wait()

    def remote(src, dst, send, recv, to):
        return pltpu.make_async_remote_copy(
            src_ref=src, dst_ref=dst, send_sem=send, recv_sem=recv, device_id=to, device_id_type=MESH
        )

    def z_copy(k, q):
        to = (s + seq - k) % seq
        return remote(
            sent.at[2 * to + q], rows.at[k, 0, c], z_send.at[k, q], z_recv.at[k, c], (d, to, q)
        )

    def z_arrival(k, q):
        return remote(sent.at[0], rows.at[k, 0, q], z_send.at[k, q], z_recv.at[k, q], (d, s, other))

    own = pltpu.make_async_copy(sent.at[2 * s + c], rows.at[0, 0, c], own_sem.at[0])
    own.start()
    z_copy(0, other).start()
    z_copy(1, 0).start()
    z_copy(1, 1).start()

    def g_x(k):
        return remote(rows.at[k, 0], rows.at[k, 1], g_send.at[k, 0], g_recv.at[k, 0], along_x)

    def g_y(k):
        return remote(rows.at[k, 0], rows.at[k, 2], g_send.at[k, 1], g_recv.at[k, 1], along_y)

    def g_xy(k):
        return remote(rows.at[k, 1, 0], rows.at[k, 3, 0], g_send.at[k, 2], g_recv.at[k, 2], along_y)

    def g_yx(k):
        return remote(rows.at[k, 2, 1], rows.at[k, 3, 1], g_send.at[k, 3], g_recv.at[k, 3], along_x)

    def r_xy(k):
        return remote(part.at[k, 3, 0], half.at[k, 0], r_send.at[k, 0], r_recv.at[k, 0], along_x)

    def r_yx(k):
        return remote(part.at[k, 3, 1], half.at[k, 1], r_send.at[k, 1], r_recv.at[k, 1], along_y)

    def r_x(k):
        return remote(part.at[k, 1, 0], sums.at[k, 0, 0], r_send.at[k, 2], r_recv.at[k, 2], along_x)

    def r_y(k):
        return remote(part.at[k, 2, 1], sums.at[k, 1, 1], r_send.at[k, 3], r_recv.at[k, 3], along_y)

    def r_x_joined(k):
        return remote(joined.at[k, 0], sums.at[k, 0, 1], r_send.at[k, 4], r_recv.at[k, 4], along_x)

    def r_y_joined(k):
        return remote(joined.at[k, 1], sums.at[k, 1, 0], r_send.at[k, 5], r_recv.at[k, 5], along_y)

    def b_copy(k, q):
        return remote(
            total.at[k, q], back.at[2 * s + c], b_send.at[k, q], b_recv.at[k, c], (d, (s + k) % seq, q)
        )

    def b_arrival(k, q):
        e = 2 * ((s + seq - k) % seq) + q
        return remote(total.at[k, q], back.at[e], b_send.at[k, q], b_recv.at[k, q], (d, s, other))

    own_back = pltpu.make_async_copy(total.at[0, c], back.at[2 * s + c], own_sem.at[1])

    def nth(t):
        return t + t // 2 - 2 * (t // 3) if seq == 4 else t

    def spread(t):
        k = nth(t)

        @pl.when(t == 0)
        def _():
            own.wait()
            z_arrival(0, other).wait_recv()

        @pl.when(t > 0)
        def _():
            z_arrival(k, 0).wait_recv()
            z_arrival(k, 1).wait_recv()

        g_x(k).start()
        g_y(k).start()

        @pl.when(jnp.logical_and(t > 0, t + 1 < seq))
        def _():
            z_copy(nth(t + 1), 0).start()
            z_copy(nth(t + 1), 1).start()

    def pass_on(k):
        g_x(k).wait_recv()
        g_xy(k).start()
        g_y(k).wait_recv()
        g_yx(k).start()

    def experts(k):
        g_xy(k).wait_recv()
        g_yx(k).wait_recv()

        @pl.when(k == nth(1))
        def _():
            for load in loads[1:]:
                load.wait()

        @pl.loop(0, hidden.shape[1] // 256)
        def _(n):
            columns = pl.ds(pl.multiple_of(n * 256, 256), 256)
            x = rows[k].reshape(8 * cap, width)
            g = jnp.dot(x, gate[:, columns], preferred_element_type=jnp.float32)
            u = jnp.dot(x, up[:, columns], preferred_element_type=jnp.float32)
            hidden[:, columns] = (g / (1.0 + jnp.exp(-g)) * u).astype(jnp.bfloat16)

        @pl.loop(0, width // 256)
        def _(n):
            columns = pl.ds(pl.multiple_of(n * 256, 256), 256)
            y = lax.dot_general(
                hidden[...],
                down[columns, :],
                (((1,), (1,)), ((), ())),
                preferred_element_type=jnp.float32,
            )
            part[k, :, :, :, columns] = y.astype(jnp.bfloat16).reshape(4, 2, cap, 256)

        r_xy(k).start()
        r_yx(k).start()
        r_x(k).start()
        r_y(k).start()

    def join(k):
        r_yx(k).wait_recv()
        joined[k, 0] = (
            part[k, 1, 1].astype(jnp.float32) + half[k, 1].astype(jnp.float32)
        ).astype(jnp.bfloat16)
        r_x_joined(k).start()
        r_xy(k).wait_recv()
        joined[k, 1] = (
            part[k, 2, 0].astype(jnp.float32) + half[k, 0].astype(jnp.float32)
        ).astype(jnp.bfloat16)
        r_y_joined(k).start()

    def give_back(k):
        r_x(k).wait_recv()
        r_y(k).wait_recv()
        r_x_joined(k).wait_recv()
        r_y_joined(k).wait_recv()
        total[k] = (
            part[k, 0].astype(jnp.float32)
            + sums[k, 0].astype(jnp.float32)
            + sums[k, 1].astype(jnp.float32)
        ).astype(jnp.bfloat16)

        @pl.when(k == 0)
        def _():
            own_back.start()
            b_copy(0, other).start()

        @pl.when(k > 0)
        def _():
            b_copy(k, 0).start()
            b_copy(k, 1).start()

    def at(t, step):
        pl.when(jnp.logical_and(t >= 0, t < seq))(lambda: step(t))

    def late(step):
        return lambda t: step(nth((t + 1) % seq))

    @pl.loop(0, seq + 5)
    def _(t):
        at(t - 1, lambda i: pass_on(nth(i)))
        at(t, spread)
        at(t - 2, late(experts))
        at(t - 3, late(join))
        at(t - 4, late(give_back))

    own_back.wait()
    b_arrival(0, other).wait_recv()
    z_copy(0, other).wait_send()
    b_copy(0, other).wait_send()
    for k in range(1, seq):
        for q in range(2):
            b_arrival(k, q).wait_recv()
            z_copy(k, q).wait_send()
            b_copy(k, q).wait_send()

    @pl.loop(0, seq)
    def _(k):
        for copy in (g_x, g_y, g_xy, g_yx, r_xy, r_yx, r_x, r_y, r_x_joined, r_y_joined):
            copy(k).wait_send()


def exchange(outgoing, gate_local, up_local, down_local):
    experts, cap, width = outgoing.shape
    seq, ff = lax.axis_size("seq"), gate_local.shape[1]
    bf16, dma = jnp.bfloat16, pltpu.SemaphoreType.DMA
    flops = 6 * 4 * experts * cap * width * ff
    return pl.pallas_call(
        functools.partial(exchange_kernel, seq),
        out_shape=jax.ShapeDtypeStruct(outgoing.shape, bf16),
        in_specs=[pl.BlockSpec(memory_space=pl.ANY)] * 4,
        out_specs=pl.BlockSpec(memory_space=pltpu.VMEM),
        scratch_shapes=[
            pltpu.VMEM(outgoing.shape, bf16),
            pltpu.VMEM(gate_local.shape, bf16),
            pltpu.VMEM(up_local.shape, bf16),
            pltpu.VMEM(down_local.shape, bf16),
            pltpu.VMEM((seq, 4, 2, cap, width), bf16),
            pltpu.VMEM((seq, 4, 2, cap, width), bf16),
            pltpu.VMEM((seq, 2, cap, width), bf16),
            pltpu.VMEM((seq, 2, cap, width), bf16),
            pltpu.VMEM((seq, 2, 2, cap, width), bf16),
            pltpu.VMEM((seq, 2, cap, width), bf16),
            pltpu.VMEM((8 * cap, ff), bf16),
            dma((4,)),
            dma((2,)),
            dma((seq, 2)),
            dma((seq, 2)),
            dma((seq, 4)),
            dma((seq, 4)),
            dma((seq, 6)),
            dma((seq, 6)),
            dma((seq, 2)),
            dma((seq, 2)),
        ],
        compiler_params=pltpu.CompilerParams(
            collective_id=0, has_side_effects=True, vmem_limit_bytes=40 << 20
        ),
        cost_estimate=pl.CostEstimate(
            flops=flops, bytes_accessed=6 * width * ff, transcendentals=4 * experts * cap * ff
        ),
    )(outgoing, gate_local, up_local, down_local)


def exchange_plain(outgoing, gate_local, up_local, down_local):
    arrived = lax.all_to_all(outgoing, ("seq", "expert"), split_axis=0, concat_axis=0, tiled=True)
    arrived_shape = arrived.shape
    shard_rows = lax.all_gather(arrived.reshape(-1, arrived_shape[2]), "dp", axis=0, tiled=True)
    gate_part = jnp.dot(shard_rows, gate_local, preferred_element_type=jnp.float32)
    up_part = jnp.dot(shard_rows, up_local, preferred_element_type=jnp.float32)
    hidden = (jax.nn.silu(gate_part) * up_part).astype(jnp.bfloat16)
    summed = lax.psum_scatter(
        lax.dot_general(
            hidden, down_local, (((1,), (1,)), ((), ())), preferred_element_type=jnp.float32
        ).astype(jnp.bfloat16),
        "dp",
        scatter_dimension=0,
        tiled=True,
    )
    served = summed.reshape(arrived_shape)
    returned_rows = lax.all_to_all(
        served, ("seq", "expert"), split_axis=0, concat_axis=0, tiled=True
    )
    return returned_rows


def local(
    frames,
    lengths,
    routes,
    norm_conv,
    point_in,
    depth_kernel,
    bn_scale,
    bn_shift,
    point_out,
    norm_moe,
    router,
    gate_weight,
    up_weight,
    down_weight,
):
    frame_rows = frames[0]
    token_count = frame_rows.shape[0]
    model_width = frame_rows.shape[1]
    position = lax.axis_index("seq") * token_count + jnp.arange(token_count, dtype=jnp.int32)
    frame_mask = (position < lengths[0]).astype(jnp.float32)[:, None]
    conv_in = layer_norm(frame_rows, norm_conv).astype(jnp.bfloat16)
    lifted = jnp.dot(conv_in, point_in, preferred_element_type=jnp.float32)
    gated = (lifted[:, :model_width] * jax.nn.sigmoid(lifted[:, model_width:]) * frame_mask).astype(
        jnp.bfloat16
    )
    reach = depth_kernel.shape[0] // 2
    padded = padded_2(gated, (("seq", 0),), reach)
    depth = jnp.zeros((token_count, model_width), jnp.float32)
    for offset in range(depth_kernel.shape[0]):
        depth = (
            depth + padded[offset : offset + token_count].astype(jnp.float32) * depth_kernel[offset]
        )
    swished = jax.nn.silu(depth * bn_scale + bn_shift).astype(jnp.bfloat16)
    residual = frame_rows.astype(jnp.float32) + jnp.dot(
        swished, point_out, preferred_element_type=jnp.float32
    )
    moe_in = layer_norm(residual, norm_moe).astype(jnp.bfloat16)
    logits = jnp.dot(moe_in, router, preferred_element_type=jnp.float32)
    seq_count = lax.axis_size("seq")
    expert_count = seq_count * lax.axis_size("expert")
    capacity = 3 * token_count // expert_count
    choice_ids = routes[0]
    expert_ids = jnp.arange(expert_count, dtype=jnp.int32)
    pick_one = (choice_ids[:, 0:1] == expert_ids[None, :]).astype(jnp.int32)
    pick_two = (choice_ids[:, 1:2] == expert_ids[None, :]).astype(jnp.int32)
    logit_one = jnp.sum(logits * pick_one.astype(jnp.float32), axis=1)
    logit_two = jnp.sum(logits * pick_two.astype(jnp.float32), axis=1)
    weight_one = jax.nn.sigmoid(logit_one - logit_two)
    weight_two = jax.nn.sigmoid(logit_two - logit_one)
    both = pick_one + pick_two
    rank = jnp.arange(token_count, dtype=jnp.int32)
    lower = (rank[:, None] > rank[None, :]).astype(jnp.bfloat16)
    earlier = jnp.dot(
        lower, both.astype(jnp.bfloat16), preferred_element_type=jnp.float32
    ).astype(jnp.int32)
    place_one = choice_ids[:, 0] * capacity + jnp.sum(earlier * pick_one, axis=1)
    place_two = choice_ids[:, 1] * capacity + jnp.sum(earlier * pick_two, axis=1)
    slot_ids = jnp.arange(expert_count * capacity, dtype=jnp.int32)
    slot_one = (place_one[:, None] == slot_ids[None, :]).astype(jnp.bfloat16)
    slot_two = (place_two[:, None] == slot_ids[None, :]).astype(jnp.bfloat16)
    outgoing = lax.dot_general(
        slot_one + slot_two, moe_in, (((0,), (0,)), ((), ())), preferred_element_type=jnp.float32
    ).astype(jnp.bfloat16)
    outgoing = outgoing.reshape(expert_count, capacity, model_width)
    gate_local = gate_weight[0]
    up_local = up_weight[0]
    down_local = down_weight[0]
    if kernel_fits(token_count, model_width, capacity, gate_local.shape[1]):
        returned_rows = exchange(outgoing, gate_local, up_local, down_local)
    else:
        returned_rows = exchange_plain(outgoing, gate_local, up_local, down_local)
    returned_rows = returned_rows.reshape(expert_count * capacity, model_width)
    from_one = jnp.dot(slot_one, returned_rows, preferred_element_type=jnp.float32)
    from_two = jnp.dot(slot_two, returned_rows, preferred_element_type=jnp.float32)
    layer_out = (
        residual + weight_one[:, None] * from_one + weight_two[:, None] * from_two
    ) * frame_mask
    return layer_out.astype(jnp.bfloat16)[None]


def solution(mesh):
    return jax.shard_map(
        local,
        mesh=mesh,
        in_specs=(
            P(("dp", "expert"), "seq", None),
            P(("dp", "expert")),
            P(("dp", "expert"), "seq", None),
            P(),
            P(),
            P(),
            P(),
            P(),
            P(),
            P(),
            P(),
            P(("seq", "expert"), None, "dp"),
            P(("seq", "expert"), None, "dp"),
            P(("seq", "expert"), None, "dp"),
        ),
        out_specs=P(("dp", "expert"), "seq", None),
        check_vma=False,
    )
```

```python
import functools
import jax
import jax.numpy as jnp
from jax import lax
from jax.experimental import pallas as pl
from jax.experimental.pallas import tpu as pltpu
from jax.sharding import PartitionSpec as P


def halo_kernel(seq, x, before, after, send_sem, recv_sem):
    d, s, c = lax.axis_index("dp"), lax.axis_index("seq"), lax.axis_index("expert")
    width, rows = before.shape[0], x.shape[0]
    left, right = (d, (s + seq - 1) % seq, c), (d, (s + 1) % seq, c)
    barrier = pltpu.get_barrier_semaphore()

    @pl.when(s > 0)
    def _():
        pl.semaphore_signal(barrier, inc=1, device_id=left, device_id_type=MESH)

    @pl.when(s < seq - 1)
    def _():
        pl.semaphore_signal(barrier, inc=1, device_id=right, device_id_type=MESH)

    pl.semaphore_wait(barrier, 2 - (seq - s) // seq - (s + 1) // seq)

    up = pltpu.make_async_remote_copy(
        src_ref=x.at[pl.ds(rows - width, width)],
        dst_ref=before,
        send_sem=send_sem.at[0],
        recv_sem=recv_sem.at[0],
        device_id=right,
        device_id_type=MESH,
    )
    down = pltpu.make_async_remote_copy(
        src_ref=x.at[pl.ds(0, width)],
        dst_ref=after,
        send_sem=send_sem.at[1],
        recv_sem=recv_sem.at[1],
        device_id=left,
        device_id_type=MESH,
    )

    @pl.when(s < seq - 1)
    def _():
        up.start()

    @pl.when(s > 0)
    def _():
        down.start()

    @pl.when(s == 0)
    def _():
        before[...] = jnp.zeros_like(before)

    @pl.when(s == seq - 1)
    def _():
        after[...] = jnp.zeros_like(after)

    @pl.when(s > 0)
    def _():
        up.wait_recv()
        down.wait_send()

    @pl.when(s < seq - 1)
    def _():
        down.wait_recv()
        up.wait_send()


def with_halo(x, reach):
    width = (reach + 15) // 16 * 16
    side = jax.ShapeDtypeStruct((width, x.shape[1]), x.dtype)
    before, after = pl.pallas_call(
        functools.partial(halo_kernel, lax.axis_size("seq")),
        out_shape=(side, side),
        in_specs=[pl.BlockSpec(memory_space=pltpu.VMEM)],
        out_specs=(pl.BlockSpec(memory_space=pltpu.VMEM),) * 2,
        scratch_shapes=[pltpu.SemaphoreType.DMA((2,)), pltpu.SemaphoreType.DMA((2,))],
        compiler_params=pltpu.CompilerParams(
            collective_id=1, has_side_effects=True, vmem_limit_bytes=4 << 20
        ),
    )(x)
    return jnp.concatenate([before[width - reach :], x, after[:reach]], axis=0)


def layer_norm(values, gain):
    values = values.astype(jnp.float32)
    center = values - jnp.mean(values, axis=-1, keepdims=True)
    spread = jnp.mean(center * center, axis=-1, keepdims=True)
    return center * lax.rsqrt(spread + 1e-05) * gain


MESH = pl.DeviceIdType.MESH


def kernel_fits(token_count, model_width, capacity, hidden):
    sizes = (lax.axis_size("dp"), lax.axis_size("expert"))
    return sizes == (4, 2) and capacity % 16 == 0 and model_width % 256 == 0 and hidden % 256 == 0


def exchange_kernel(
    seq,
    out_hbm,
    gate_hbm,
    up_hbm,
    down_hbm,
    back,
    sent,
    gate,
    up,
    down,
    rows,
    part,
    half,
    joined,
    sums,
    total,
    hidden,
    load_sem,
    own_sem,
    z_send,
    z_recv,
    g_send,
    g_recv,
    r_send,
    r_recv,
    b_send,
    b_recv,
):
    d, s, c = lax.axis_index("dp"), lax.axis_index("seq"), lax.axis_index("expert")
    other = 1 - c
    cap, width = rows.shape[3], rows.shape[4]
    along_x = (d // 2 * 2 + (1 - d % 2), s, c)
    along_y = ((d + 2) % 4, s, c)
    loads = [
        pltpu.make_async_copy(out_hbm, sent, load_sem.at[0]),
        pltpu.make_async_copy(gate_hbm, gate, load_sem.at[1]),
        pltpu.make_async_copy(up_hbm, up, load_sem.at[2]),
        pltpu.make_async_copy(down_hbm, down, load_sem.at[3]),
    ]
    for load in loads:
        load.start()

    barrier = pltpu.get_barrier_semaphore()
    peers = [along_x, along_y, (d, s, other)]
    for k in range(1, seq):
        peers += [(d, (s + k) % seq, 0), (d, (s + k) % seq, 1)]
    for peer in peers:
        pl.semaphore_signal(barrier, inc=1, device_id=peer, device_id_type=MESH)
    pl.semaphore_wait(barrier, len(peers))
    loads[0].wait()

    def remote(src, dst, send, recv, to):
        return pltpu.make_async_remote_copy(
            src_ref=src, dst_ref=dst, send_sem=send, recv_sem=recv, device_id=to, device_id_type=MESH
        )

    def z_copy(k, q):
        to = (s + seq - k) % seq
        return remote(
            sent.at[2 * to + q], rows.at[k, 0, c], z_send.at[k, q], z_recv.at[k, c], (d, to, q)
        )

    def z_arrival(k, q):
        return remote(sent.at[0], rows.at[k, 0, q], z_send.at[k, q], z_recv.at[k, q], (d, s, other))

    own = pltpu.make_async_copy(sent.at[2 * s + c], rows.at[0, 0, c], own_sem.at[0])
    own.start()
    z_copy(0, other).start()
    z_copy(1, 0).start()
    z_copy(1, 1).start()

    def g_x(k):
        return remote(rows.at[k, 0], rows.at[k, 1], g_send.at[k, 0], g_recv.at[k, 0], along_x)

    def g_y(k):
        return remote(rows.at[k, 0], rows.at[k, 2], g_send.at[k, 1], g_recv.at[k, 1], along_y)

    def g_xy(k):
        return remote(rows.at[k, 1, 0], rows.at[k, 3, 0], g_send.at[k, 2], g_recv.at[k, 2], along_y)

    def g_yx(k):
        return remote(rows.at[k, 2, 1], rows.at[k, 3, 1], g_send.at[k, 3], g_recv.at[k, 3], along_x)

    def r_xy(k):
        return remote(part.at[k, 3, 0], half.at[k, 0], r_send.at[k, 0], r_recv.at[k, 0], along_x)

    def r_yx(k):
        return remote(part.at[k, 3, 1], half.at[k, 1], r_send.at[k, 1], r_recv.at[k, 1], along_y)

    def r_x(k):
        return remote(part.at[k, 1, 0], sums.at[k, 0, 0], r_send.at[k, 2], r_recv.at[k, 2], along_x)

    def r_y(k):
        return remote(part.at[k, 2, 1], sums.at[k, 1, 1], r_send.at[k, 3], r_recv.at[k, 3], along_y)

    def r_x_joined(k):
        return remote(joined.at[k, 0], sums.at[k, 0, 1], r_send.at[k, 4], r_recv.at[k, 4], along_x)

    def r_y_joined(k):
        return remote(joined.at[k, 1], sums.at[k, 1, 0], r_send.at[k, 5], r_recv.at[k, 5], along_y)

    def b_copy(k, q):
        return remote(
            total.at[k, q], back.at[2 * s + c], b_send.at[k, q], b_recv.at[k, c], (d, (s + k) % seq, q)
        )

    def b_arrival(k, q):
        e = 2 * ((s + seq - k) % seq) + q
        return remote(total.at[k, q], back.at[e], b_send.at[k, q], b_recv.at[k, q], (d, s, other))

    own_back = pltpu.make_async_copy(total.at[0, c], back.at[2 * s + c], own_sem.at[1])

    def nth(t):
        return t + t // 2 - 2 * (t // 3) if seq == 4 else t

    def spread(t):
        k = nth(t)

        @pl.when(t == 0)
        def _():
            own.wait()
            z_arrival(0, other).wait_recv()

        @pl.when(t > 0)
        def _():
            z_arrival(k, 0).wait_recv()
            z_arrival(k, 1).wait_recv()

        g_x(k).start()
        g_y(k).start()

        @pl.when(jnp.logical_and(t > 0, t + 1 < seq))
        def _():
            z_copy(nth(t + 1), 0).start()
            z_copy(nth(t + 1), 1).start()

    def pass_on(k):
        g_x(k).wait_recv()
        g_xy(k).start()
        g_y(k).wait_recv()
        g_yx(k).start()

    def experts(k):
        g_xy(k).wait_recv()
        g_yx(k).wait_recv()

        @pl.when(k == nth(1))
        def _():
            for load in loads[1:]:
                load.wait()

        @pl.loop(0, hidden.shape[1] // 256)
        def _(n):
            columns = pl.ds(pl.multiple_of(n * 256, 256), 256)
            x = rows[k].reshape(8 * cap, width)
            g = jnp.dot(x, gate[:, columns], preferred_element_type=jnp.float32)
            u = jnp.dot(x, up[:, columns], preferred_element_type=jnp.float32)
            hidden[:, columns] = (g / (1.0 + jnp.exp(-g)) * u).astype(jnp.bfloat16)

        @pl.loop(0, width // 256)
        def _(n):
            columns = pl.ds(pl.multiple_of(n * 256, 256), 256)
            y = lax.dot_general(
                hidden[...],
                down[columns, :],
                (((1,), (1,)), ((), ())),
                preferred_element_type=jnp.float32,
            )
            part[k, :, :, :, columns] = y.astype(jnp.bfloat16).reshape(4, 2, cap, 256)

        r_xy(k).start()
        r_yx(k).start()
        r_x(k).start()
        r_y(k).start()

    def join(k):
        r_yx(k).wait_recv()
        joined[k, 0] = (
            part[k, 1, 1].astype(jnp.float32) + half[k, 1].astype(jnp.float32)
        ).astype(jnp.bfloat16)
        r_x_joined(k).start()
        r_xy(k).wait_recv()
        joined[k, 1] = (
            part[k, 2, 0].astype(jnp.float32) + half[k, 0].astype(jnp.float32)
        ).astype(jnp.bfloat16)
        r_y_joined(k).start()

    def give_back(k):
        r_x(k).wait_recv()
        r_y(k).wait_recv()
        r_x_joined(k).wait_recv()
        r_y_joined(k).wait_recv()
        total[k] = (
            part[k, 0].astype(jnp.float32)
            + sums[k, 0].astype(jnp.float32)
            + sums[k, 1].astype(jnp.float32)
        ).astype(jnp.bfloat16)

        @pl.when(k == 0)
        def _():
            own_back.start()
            b_copy(0, other).start()

        @pl.when(k > 0)
        def _():
            b_copy(k, 0).start()
            b_copy(k, 1).start()

    def at(t, step):
        pl.when(jnp.logical_and(t >= 0, t < seq))(lambda: step(t))

    def late(step):
        return lambda t: step(nth((t + 1) % seq))

    @pl.loop(0, seq + 5)
    def _(t):
        at(t - 1, lambda i: pass_on(nth(i)))
        at(t, spread)
        at(t - 2, late(experts))
        at(t - 3, late(join))
        at(t - 4, late(give_back))

    own_back.wait()
    b_arrival(0, other).wait_recv()
    z_copy(0, other).wait_send()
    b_copy(0, other).wait_send()
    for k in range(1, seq):
        for q in range(2):
            b_arrival(k, q).wait_recv()
            z_copy(k, q).wait_send()
            b_copy(k, q).wait_send()

    @pl.loop(0, seq)
    def _(k):
        for copy in (g_x, g_y, g_xy, g_yx, r_xy, r_yx, r_x, r_y, r_x_joined, r_y_joined):
            copy(k).wait_send()


def exchange(outgoing, gate_local, up_local, down_local):
    experts, cap, width = outgoing.shape
    seq, ff = lax.axis_size("seq"), gate_local.shape[1]
    bf16, dma = jnp.bfloat16, pltpu.SemaphoreType.DMA
    flops = 6 * 4 * experts * cap * width * ff
    return pl.pallas_call(
        functools.partial(exchange_kernel, seq),
        out_shape=jax.ShapeDtypeStruct(outgoing.shape, bf16),
        in_specs=[pl.BlockSpec(memory_space=pl.ANY)] * 4,
        out_specs=pl.BlockSpec(memory_space=pltpu.VMEM),
        scratch_shapes=[
            pltpu.VMEM(outgoing.shape, bf16),
            pltpu.VMEM(gate_local.shape, bf16),
            pltpu.VMEM(up_local.shape, bf16),
            pltpu.VMEM(down_local.shape, bf16),
            pltpu.VMEM((seq, 4, 2, cap, width), bf16),
            pltpu.VMEM((seq, 4, 2, cap, width), bf16),
            pltpu.VMEM((seq, 2, cap, width), bf16),
            pltpu.VMEM((seq, 2, cap, width), bf16),
            pltpu.VMEM((seq, 2, 2, cap, width), bf16),
            pltpu.VMEM((seq, 2, cap, width), bf16),
            pltpu.VMEM((8 * cap, ff), bf16),
            dma((4,)),
            dma((2,)),
            dma((seq, 2)),
            dma((seq, 2)),
            dma((seq, 4)),
            dma((seq, 4)),
            dma((seq, 6)),
            dma((seq, 6)),
            dma((seq, 2)),
            dma((seq, 2)),
        ],
        compiler_params=pltpu.CompilerParams(
            collective_id=0, has_side_effects=True, vmem_limit_bytes=40 << 20
        ),
        cost_estimate=pl.CostEstimate(
            flops=flops, bytes_accessed=6 * width * ff, transcendentals=4 * experts * cap * ff
        ),
    )(outgoing, gate_local, up_local, down_local)


def exchange_plain(outgoing, gate_local, up_local, down_local):
    arrived = lax.all_to_all(outgoing, ("seq", "expert"), split_axis=0, concat_axis=0, tiled=True)
    arrived_shape = arrived.shape
    shard_rows = lax.all_gather(arrived.reshape(-1, arrived_shape[2]), "dp", axis=0, tiled=True)
    gate_part = jnp.dot(shard_rows, gate_local, preferred_element_type=jnp.float32)
    up_part = jnp.dot(shard_rows, up_local, preferred_element_type=jnp.float32)
    hidden = (jax.nn.silu(gate_part) * up_part).astype(jnp.bfloat16)
    summed = lax.psum_scatter(
        lax.dot_general(
            hidden, down_local, (((1,), (1,)), ((), ())), preferred_element_type=jnp.float32
        ).astype(jnp.bfloat16),
        "dp",
        scatter_dimension=0,
        tiled=True,
    )
    served = summed.reshape(arrived_shape)
    returned_rows = lax.all_to_all(
        served, ("seq", "expert"), split_axis=0, concat_axis=0, tiled=True
    )
    return returned_rows


def local(
    frames,
    lengths,
    routes,
    norm_conv,
    point_in,
    depth_kernel,
    bn_scale,
    bn_shift,
    point_out,
    norm_moe,
    router,
    gate_weight,
    up_weight,
    down_weight,
):
    frame_rows = frames[0]
    token_count = frame_rows.shape[0]
    model_width = frame_rows.shape[1]
    position = lax.axis_index("seq") * token_count + jnp.arange(token_count, dtype=jnp.int32)
    frame_mask = (position < lengths[0]).astype(jnp.float32)[:, None]
    conv_in = layer_norm(frame_rows, norm_conv).astype(jnp.bfloat16)
    lifted = jnp.dot(conv_in, point_in, preferred_element_type=jnp.float32)
    gated = (lifted[:, :model_width] * jax.nn.sigmoid(lifted[:, model_width:]) * frame_mask).astype(
        jnp.bfloat16
    )
    reach = depth_kernel.shape[0] // 2
    padded = with_halo(gated, reach)
    depth = jnp.zeros((token_count, model_width), jnp.float32)
    for offset in range(depth_kernel.shape[0]):
        depth = (
            depth + padded[offset : offset + token_count].astype(jnp.float32) * depth_kernel[offset]
        )
    swished = jax.nn.silu(depth * bn_scale + bn_shift).astype(jnp.bfloat16)
    residual = frame_rows.astype(jnp.float32) + jnp.dot(
        swished, point_out, preferred_element_type=jnp.float32
    )
    moe_in = layer_norm(residual, norm_moe).astype(jnp.bfloat16)
    logits = jnp.dot(moe_in, router, preferred_element_type=jnp.float32)
    seq_count = lax.axis_size("seq")
    expert_count = seq_count * lax.axis_size("expert")
    capacity = 3 * token_count // expert_count
    choice_ids = routes[0]
    expert_ids = jnp.arange(expert_count, dtype=jnp.int32)
    pick_one = (choice_ids[:, 0:1] == expert_ids[None, :]).astype(jnp.int32)
    pick_two = (choice_ids[:, 1:2] == expert_ids[None, :]).astype(jnp.int32)
    logit_one = jnp.sum(logits * pick_one.astype(jnp.float32), axis=1)
    logit_two = jnp.sum(logits * pick_two.astype(jnp.float32), axis=1)
    weight_one = jax.nn.sigmoid(logit_one - logit_two)
    weight_two = jax.nn.sigmoid(logit_two - logit_one)
    both = pick_one + pick_two
    rank = jnp.arange(token_count, dtype=jnp.int32)
    lower = (rank[:, None] > rank[None, :]).astype(jnp.bfloat16)
    earlier = jnp.dot(
        lower, both.astype(jnp.bfloat16), preferred_element_type=jnp.float32
    ).astype(jnp.int32)
    place_one = choice_ids[:, 0] * capacity + jnp.sum(earlier * pick_one, axis=1)
    place_two = choice_ids[:, 1] * capacity + jnp.sum(earlier * pick_two, axis=1)
    slot_ids = jnp.arange(expert_count * capacity, dtype=jnp.int32)
    slot_one = (place_one[:, None] == slot_ids[None, :]).astype(jnp.bfloat16)
    slot_two = (place_two[:, None] == slot_ids[None, :]).astype(jnp.bfloat16)
    outgoing = lax.dot_general(
        slot_one + slot_two, moe_in, (((0,), (0,)), ((), ())), preferred_element_type=jnp.float32
    ).astype(jnp.bfloat16)
    outgoing = outgoing.reshape(expert_count, capacity, model_width)
    gate_local = gate_weight[0]
    up_local = up_weight[0]
    down_local = down_weight[0]
    if kernel_fits(token_count, model_width, capacity, gate_local.shape[1]):
        returned_rows = exchange(outgoing, gate_local, up_local, down_local)
    else:
        returned_rows = exchange_plain(outgoing, gate_local, up_local, down_local)
    returned_rows = returned_rows.reshape(expert_count * capacity, model_width)
    from_one = jnp.dot(slot_one, returned_rows, preferred_element_type=jnp.float32)
    from_two = jnp.dot(slot_two, returned_rows, preferred_element_type=jnp.float32)
    layer_out = (
        residual + weight_one[:, None] * from_one + weight_two[:, None] * from_two
    ) * frame_mask
    return layer_out.astype(jnp.bfloat16)[None]


def solution(mesh):
    return jax.shard_map(
        local,
        mesh=mesh,
        in_specs=(
            P(("dp", "expert"), "seq", None),
            P(("dp", "expert")),
            P(("dp", "expert"), "seq", None),
            P(),
            P(),
            P(),
            P(),
            P(),
            P(),
            P(),
            P(),
            P(("seq", "expert"), None, "dp"),
            P(("seq", "expert"), None, "dp"),
            P(("seq", "expert"), None, "dp"),
        ),
        out_specs=P(("dp", "expert"), "seq", None),
        check_vma=False,
    )
```

```python
import functools
import jax
import jax.numpy as jnp
from jax import lax
from jax.experimental import pallas as pl
from jax.experimental.pallas import tpu as pltpu
from jax.sharding import PartitionSpec as P


def halo_kernel(seq, x, taps, scale, shift, out, before, after, padded, send_sem, recv_sem):
    d, s, c = lax.axis_index("dp"), lax.axis_index("seq"), lax.axis_index("expert")
    width, rows = before.shape[0], x.shape[0]
    left, right = (d, (s + seq - 1) % seq, c), (d, (s + 1) % seq, c)
    barrier = pltpu.get_barrier_semaphore()

    @pl.when(s > 0)
    def _():
        pl.semaphore_signal(barrier, inc=1, device_id=left, device_id_type=MESH)

    @pl.when(s < seq - 1)
    def _():
        pl.semaphore_signal(barrier, inc=1, device_id=right, device_id_type=MESH)

    pl.semaphore_wait(barrier, 2 - (seq - s) // seq - (s + 1) // seq)

    up = pltpu.make_async_remote_copy(
        src_ref=x.at[pl.ds(rows - width, width)],
        dst_ref=before,
        send_sem=send_sem.at[0],
        recv_sem=recv_sem.at[0],
        device_id=right,
        device_id_type=MESH,
    )
    down = pltpu.make_async_remote_copy(
        src_ref=x.at[pl.ds(0, width)],
        dst_ref=after,
        send_sem=send_sem.at[1],
        recv_sem=recv_sem.at[1],
        device_id=left,
        device_id_type=MESH,
    )

    @pl.when(s < seq - 1)
    def _():
        up.start()

    @pl.when(s > 0)
    def _():
        down.start()

    @pl.when(s == 0)
    def _():
        before[...] = jnp.zeros_like(before)

    @pl.when(s == seq - 1)
    def _():
        after[...] = jnp.zeros_like(after)

    padded[pl.ds(width, rows), :] = x[...].astype(jnp.float32)

    @pl.when(s > 0)
    def _():
        up.wait_recv()
        down.wait_send()

    @pl.when(s < seq - 1)
    def _():
        down.wait_recv()
        up.wait_send()

    padded[pl.ds(0, width), :] = before[...].astype(jnp.float32)
    padded[pl.ds(width + rows, width), :] = after[...].astype(jnp.float32)
    reach = taps.shape[0] // 2

    @pl.loop(0, x.shape[1] // 128)
    def _(n):
        columns = pl.ds(pl.multiple_of(n * 128, 128), 128)
        depth = jnp.zeros((rows, 128), jnp.float32)
        for t in range(taps.shape[0]):
            depth += padded[pl.ds(width - reach + t, rows), columns] * taps[pl.ds(t, 1), columns]
        v = depth * scale[:, columns] + shift[:, columns]
        out[:, columns] = (v / (1.0 + jnp.exp(-v))).astype(jnp.bfloat16)


def depthwise(x, taps, scale, shift):
    rows, features = x.shape
    width = (taps.shape[0] // 2 + 15) // 16 * 16
    dma = pltpu.SemaphoreType.DMA
    return pl.pallas_call(
        functools.partial(halo_kernel, lax.axis_size("seq")),
        out_shape=jax.ShapeDtypeStruct(x.shape, x.dtype),
        in_specs=[pl.BlockSpec(memory_space=pltpu.VMEM)] * 4,
        out_specs=pl.BlockSpec(memory_space=pltpu.VMEM),
        scratch_shapes=[
            pltpu.VMEM((width, features), x.dtype),
            pltpu.VMEM((width, features), x.dtype),
            pltpu.VMEM((rows + 2 * width, features), jnp.float32),
            dma((2,)),
            dma((2,)),
        ],
        compiler_params=pltpu.CompilerParams(
            collective_id=1, has_side_effects=True, vmem_limit_bytes=8 << 20
        ),
    )(x, taps, scale[None, :], shift[None, :])


def layer_norm(values, gain):
    values = values.astype(jnp.float32)
    center = values - jnp.mean(values, axis=-1, keepdims=True)
    spread = jnp.mean(center * center, axis=-1, keepdims=True)
    return center * lax.rsqrt(spread + 1e-05) * gain


MESH = pl.DeviceIdType.MESH


def kernel_fits(token_count, model_width, capacity, hidden):
    sizes = (lax.axis_size("dp"), lax.axis_size("expert"))
    return sizes == (4, 2) and capacity % 16 == 0 and model_width % 256 == 0 and hidden % 256 == 0


def exchange_kernel(
    seq,
    out_hbm,
    gate_hbm,
    up_hbm,
    down_hbm,
    back,
    sent,
    gate,
    up,
    down,
    rows,
    part,
    half,
    joined,
    sums,
    total,
    hidden,
    load_sem,
    own_sem,
    z_send,
    z_recv,
    g_send,
    g_recv,
    r_send,
    r_recv,
    b_send,
    b_recv,
):
    d, s, c = lax.axis_index("dp"), lax.axis_index("seq"), lax.axis_index("expert")
    other = 1 - c
    cap, width = rows.shape[3], rows.shape[4]
    along_x = (d // 2 * 2 + (1 - d % 2), s, c)
    along_y = ((d + 2) % 4, s, c)
    loads = [
        pltpu.make_async_copy(out_hbm, sent, load_sem.at[0]),
        pltpu.make_async_copy(gate_hbm, gate, load_sem.at[1]),
        pltpu.make_async_copy(up_hbm, up, load_sem.at[2]),
        pltpu.make_async_copy(down_hbm, down, load_sem.at[3]),
    ]
    for load in loads:
        load.start()

    barrier = pltpu.get_barrier_semaphore()
    peers = [along_x, along_y, (d, s, other)]
    for k in range(1, seq):
        peers += [(d, (s + k) % seq, 0), (d, (s + k) % seq, 1)]
    for peer in peers:
        pl.semaphore_signal(barrier, inc=1, device_id=peer, device_id_type=MESH)
    pl.semaphore_wait(barrier, len(peers))
    loads[0].wait()

    def remote(src, dst, send, recv, to):
        return pltpu.make_async_remote_copy(
            src_ref=src, dst_ref=dst, send_sem=send, recv_sem=recv, device_id=to, device_id_type=MESH
        )

    def z_copy(k, q):
        to = (s + seq - k) % seq
        return remote(
            sent.at[2 * to + q], rows.at[k, 0, c], z_send.at[k, q], z_recv.at[k, c], (d, to, q)
        )

    def z_arrival(k, q):
        return remote(sent.at[0], rows.at[k, 0, q], z_send.at[k, q], z_recv.at[k, q], (d, s, other))

    own = pltpu.make_async_copy(sent.at[2 * s + c], rows.at[0, 0, c], own_sem.at[0])
    own.start()
    z_copy(0, other).start()
    z_copy(1, 0).start()
    z_copy(1, 1).start()

    def g_x(k):
        return remote(rows.at[k, 0], rows.at[k, 1], g_send.at[k, 0], g_recv.at[k, 0], along_x)

    def g_y(k):
        return remote(rows.at[k, 0], rows.at[k, 2], g_send.at[k, 1], g_recv.at[k, 1], along_y)

    def g_xy(k):
        return remote(rows.at[k, 1, 0], rows.at[k, 3, 0], g_send.at[k, 2], g_recv.at[k, 2], along_y)

    def g_yx(k):
        return remote(rows.at[k, 2, 1], rows.at[k, 3, 1], g_send.at[k, 3], g_recv.at[k, 3], along_x)

    def r_xy(k):
        return remote(part.at[k, 3, 0], half.at[k, 0], r_send.at[k, 0], r_recv.at[k, 0], along_x)

    def r_yx(k):
        return remote(part.at[k, 3, 1], half.at[k, 1], r_send.at[k, 1], r_recv.at[k, 1], along_y)

    def r_x(k):
        return remote(part.at[k, 1, 0], sums.at[k, 0, 0], r_send.at[k, 2], r_recv.at[k, 2], along_x)

    def r_y(k):
        return remote(part.at[k, 2, 1], sums.at[k, 1, 1], r_send.at[k, 3], r_recv.at[k, 3], along_y)

    def r_x_joined(k):
        return remote(joined.at[k, 0], sums.at[k, 0, 1], r_send.at[k, 4], r_recv.at[k, 4], along_x)

    def r_y_joined(k):
        return remote(joined.at[k, 1], sums.at[k, 1, 0], r_send.at[k, 5], r_recv.at[k, 5], along_y)

    def b_copy(k, q):
        return remote(
            total.at[k, q], back.at[2 * s + c], b_send.at[k, q], b_recv.at[k, c], (d, (s + k) % seq, q)
        )

    def b_arrival(k, q):
        e = 2 * ((s + seq - k) % seq) + q
        return remote(total.at[k, q], back.at[e], b_send.at[k, q], b_recv.at[k, q], (d, s, other))

    own_back = pltpu.make_async_copy(total.at[0, c], back.at[2 * s + c], own_sem.at[1])

    def nth(t):
        return t + t // 2 - 2 * (t // 3) if seq == 4 else t

    def spread(t):
        k = nth(t)

        @pl.when(t == 0)
        def _():
            own.wait()
            z_arrival(0, other).wait_recv()

        @pl.when(t > 0)
        def _():
            z_arrival(k, 0).wait_recv()
            z_arrival(k, 1).wait_recv()

        g_x(k).start()
        g_y(k).start()

        @pl.when(jnp.logical_and(t > 0, t + 1 < seq))
        def _():
            z_copy(nth(t + 1), 0).start()
            z_copy(nth(t + 1), 1).start()

    def pass_on(k):
        g_x(k).wait_recv()
        g_xy(k).start()
        g_y(k).wait_recv()
        g_yx(k).start()

    def experts(k):
        g_xy(k).wait_recv()
        g_yx(k).wait_recv()

        @pl.when(k == nth(1))
        def _():
            for load in loads[1:]:
                load.wait()

        @pl.loop(0, hidden.shape[1] // 256)
        def _(n):
            columns = pl.ds(pl.multiple_of(n * 256, 256), 256)
            x = rows[k].reshape(8 * cap, width)
            g = jnp.dot(x, gate[:, columns], preferred_element_type=jnp.float32)
            u = jnp.dot(x, up[:, columns], preferred_element_type=jnp.float32)
            hidden[:, columns] = (g / (1.0 + jnp.exp(-g)) * u).astype(jnp.bfloat16)

        @pl.loop(0, width // 256)
        def _(n):
            columns = pl.ds(pl.multiple_of(n * 256, 256), 256)
            y = lax.dot_general(
                hidden[...],
                down[columns, :],
                (((1,), (1,)), ((), ())),
                preferred_element_type=jnp.float32,
            )
            part[k, :, :, :, columns] = y.astype(jnp.bfloat16).reshape(4, 2, cap, 256)

        r_xy(k).start()
        r_yx(k).start()
        r_x(k).start()
        r_y(k).start()

    def join(k):
        r_yx(k).wait_recv()
        joined[k, 0] = (
            part[k, 1, 1].astype(jnp.float32) + half[k, 1].astype(jnp.float32)
        ).astype(jnp.bfloat16)
        r_x_joined(k).start()
        r_xy(k).wait_recv()
        joined[k, 1] = (
            part[k, 2, 0].astype(jnp.float32) + half[k, 0].astype(jnp.float32)
        ).astype(jnp.bfloat16)
        r_y_joined(k).start()

    def give_back(k):
        r_x(k).wait_recv()
        r_y(k).wait_recv()
        r_x_joined(k).wait_recv()
        r_y_joined(k).wait_recv()
        total[k] = (
            part[k, 0].astype(jnp.float32)
            + sums[k, 0].astype(jnp.float32)
            + sums[k, 1].astype(jnp.float32)
        ).astype(jnp.bfloat16)

        @pl.when(k == 0)
        def _():
            own_back.start()
            b_copy(0, other).start()

        @pl.when(k > 0)
        def _():
            b_copy(k, 0).start()
            b_copy(k, 1).start()

    def at(t, step):
        pl.when(jnp.logical_and(t >= 0, t < seq))(lambda: step(t))

    def late(step):
        return lambda t: step(nth((t + 1) % seq))

    @pl.loop(0, seq + 5)
    def _(t):
        at(t - 1, lambda i: pass_on(nth(i)))
        at(t, spread)
        at(t - 2, late(experts))
        at(t - 3, late(join))
        at(t - 4, late(give_back))

    own_back.wait()
    b_arrival(0, other).wait_recv()
    z_copy(0, other).wait_send()
    b_copy(0, other).wait_send()
    for k in range(1, seq):
        for q in range(2):
            b_arrival(k, q).wait_recv()
            z_copy(k, q).wait_send()
            b_copy(k, q).wait_send()

    @pl.loop(0, seq)
    def _(k):
        for copy in (g_x, g_y, g_xy, g_yx, r_xy, r_yx, r_x, r_y, r_x_joined, r_y_joined):
            copy(k).wait_send()


def exchange(outgoing, gate_local, up_local, down_local):
    experts, cap, width = outgoing.shape
    seq, ff = lax.axis_size("seq"), gate_local.shape[1]
    bf16, dma = jnp.bfloat16, pltpu.SemaphoreType.DMA
    flops = 6 * 4 * experts * cap * width * ff
    return pl.pallas_call(
        functools.partial(exchange_kernel, seq),
        out_shape=jax.ShapeDtypeStruct(outgoing.shape, bf16),
        in_specs=[pl.BlockSpec(memory_space=pl.ANY)] * 4,
        out_specs=pl.BlockSpec(memory_space=pltpu.VMEM),
        scratch_shapes=[
            pltpu.VMEM(outgoing.shape, bf16),
            pltpu.VMEM(gate_local.shape, bf16),
            pltpu.VMEM(up_local.shape, bf16),
            pltpu.VMEM(down_local.shape, bf16),
            pltpu.VMEM((seq, 4, 2, cap, width), bf16),
            pltpu.VMEM((seq, 4, 2, cap, width), bf16),
            pltpu.VMEM((seq, 2, cap, width), bf16),
            pltpu.VMEM((seq, 2, cap, width), bf16),
            pltpu.VMEM((seq, 2, 2, cap, width), bf16),
            pltpu.VMEM((seq, 2, cap, width), bf16),
            pltpu.VMEM((8 * cap, ff), bf16),
            dma((4,)),
            dma((2,)),
            dma((seq, 2)),
            dma((seq, 2)),
            dma((seq, 4)),
            dma((seq, 4)),
            dma((seq, 6)),
            dma((seq, 6)),
            dma((seq, 2)),
            dma((seq, 2)),
        ],
        compiler_params=pltpu.CompilerParams(
            collective_id=0, has_side_effects=True, vmem_limit_bytes=40 << 20
        ),
        cost_estimate=pl.CostEstimate(
            flops=flops, bytes_accessed=6 * width * ff, transcendentals=4 * experts * cap * ff
        ),
    )(outgoing, gate_local, up_local, down_local)


def exchange_plain(outgoing, gate_local, up_local, down_local):
    arrived = lax.all_to_all(outgoing, ("seq", "expert"), split_axis=0, concat_axis=0, tiled=True)
    arrived_shape = arrived.shape
    shard_rows = lax.all_gather(arrived.reshape(-1, arrived_shape[2]), "dp", axis=0, tiled=True)
    gate_part = jnp.dot(shard_rows, gate_local, preferred_element_type=jnp.float32)
    up_part = jnp.dot(shard_rows, up_local, preferred_element_type=jnp.float32)
    hidden = (jax.nn.silu(gate_part) * up_part).astype(jnp.bfloat16)
    summed = lax.psum_scatter(
        lax.dot_general(
            hidden, down_local, (((1,), (1,)), ((), ())), preferred_element_type=jnp.float32
        ).astype(jnp.bfloat16),
        "dp",
        scatter_dimension=0,
        tiled=True,
    )
    served = summed.reshape(arrived_shape)
    returned_rows = lax.all_to_all(
        served, ("seq", "expert"), split_axis=0, concat_axis=0, tiled=True
    )
    return returned_rows


def local(
    frames,
    lengths,
    routes,
    norm_conv,
    point_in,
    depth_kernel,
    bn_scale,
    bn_shift,
    point_out,
    norm_moe,
    router,
    gate_weight,
    up_weight,
    down_weight,
):
    frame_rows = frames[0]
    token_count = frame_rows.shape[0]
    model_width = frame_rows.shape[1]
    position = lax.axis_index("seq") * token_count + jnp.arange(token_count, dtype=jnp.int32)
    frame_mask = (position < lengths[0]).astype(jnp.float32)[:, None]
    conv_in = layer_norm(frame_rows, norm_conv).astype(jnp.bfloat16)
    lifted = jnp.dot(conv_in, point_in, preferred_element_type=jnp.float32)
    gated = (lifted[:, :model_width] * jax.nn.sigmoid(lifted[:, model_width:]) * frame_mask).astype(
        jnp.bfloat16
    )
    swished = depthwise(gated, depth_kernel, bn_scale, bn_shift)
    residual = frame_rows.astype(jnp.float32) + jnp.dot(
        swished, point_out, preferred_element_type=jnp.float32
    )
    moe_in = layer_norm(residual, norm_moe).astype(jnp.bfloat16)
    logits = jnp.dot(moe_in, router, preferred_element_type=jnp.float32)
    seq_count = lax.axis_size("seq")
    expert_count = seq_count * lax.axis_size("expert")
    capacity = 3 * token_count // expert_count
    choice_ids = routes[0]
    expert_ids = jnp.arange(expert_count, dtype=jnp.int32)
    pick_one = (choice_ids[:, 0:1] == expert_ids[None, :]).astype(jnp.int32)
    pick_two = (choice_ids[:, 1:2] == expert_ids[None, :]).astype(jnp.int32)
    logit_one = jnp.sum(logits * pick_one.astype(jnp.float32), axis=1)
    logit_two = jnp.sum(logits * pick_two.astype(jnp.float32), axis=1)
    weight_one = jax.nn.sigmoid(logit_one - logit_two)
    weight_two = jax.nn.sigmoid(logit_two - logit_one)
    both = pick_one + pick_two
    rank = jnp.arange(token_count, dtype=jnp.int32)
    lower = (rank[:, None] > rank[None, :]).astype(jnp.bfloat16)
    earlier = jnp.dot(
        lower, both.astype(jnp.bfloat16), preferred_element_type=jnp.float32
    ).astype(jnp.int32)
    place_one = choice_ids[:, 0] * capacity + jnp.sum(earlier * pick_one, axis=1)
    place_two = choice_ids[:, 1] * capacity + jnp.sum(earlier * pick_two, axis=1)
    slot_ids = jnp.arange(expert_count * capacity, dtype=jnp.int32)
    slot_one = (place_one[:, None] == slot_ids[None, :]).astype(jnp.bfloat16)
    slot_two = (place_two[:, None] == slot_ids[None, :]).astype(jnp.bfloat16)
    outgoing = lax.dot_general(
        slot_one + slot_two, moe_in, (((0,), (0,)), ((), ())), preferred_element_type=jnp.float32
    ).astype(jnp.bfloat16)
    outgoing = outgoing.reshape(expert_count, capacity, model_width)
    gate_local = gate_weight[0]
    up_local = up_weight[0]
    down_local = down_weight[0]
    if kernel_fits(token_count, model_width, capacity, gate_local.shape[1]):
        returned_rows = exchange(outgoing, gate_local, up_local, down_local)
    else:
        returned_rows = exchange_plain(outgoing, gate_local, up_local, down_local)
    returned_rows = returned_rows.reshape(expert_count * capacity, model_width)
    from_one = jnp.dot(slot_one, returned_rows, preferred_element_type=jnp.float32)
    from_two = jnp.dot(slot_two, returned_rows, preferred_element_type=jnp.float32)
    layer_out = (
        residual + weight_one[:, None] * from_one + weight_two[:, None] * from_two
    ) * frame_mask
    return layer_out.astype(jnp.bfloat16)[None]


def solution(mesh):
    return jax.shard_map(
        local,
        mesh=mesh,
        in_specs=(
            P(("dp", "expert"), "seq", None),
            P(("dp", "expert")),
            P(("dp", "expert"), "seq", None),
            P(),
            P(),
            P(),
            P(),
            P(),
            P(),
            P(),
            P(),
            P(("seq", "expert"), None, "dp"),
            P(("seq", "expert"), None, "dp"),
            P(("seq", "expert"), None, "dp"),
        ),
        out_specs=P(("dp", "expert"), "seq", None),
        check_vma=False,
    )
```
